32 devices in a mesh: groups: 2 (over y), patch: 4 (over x, core), tensor: 4 (over z).
Axes of the slice: x: 2, y: 2, z: 4, core: 2. Of those that a mesh axis runs over, the one named last changes fastest.
Arguments:
- source: bfloat16 [8192, 69, 128], P(('groups', 'patch', 'tensor')), parts along dimension 0, may hold values from -48 to 48
- intersection_tiles: bfloat16 [4096, 2, 128, 128], P(('patch', 'tensor')), may hold values from 0.0009994507 to 1
- send_index: int32 [16, 16, 2], P(('patch', 'tensor')), may hold values from 0 to 255, as said below
- intersection: int32 [4096, 2], P(('patch', 'tensor')), may hold values from 0 to 31, as said below
- emb_weight: bfloat16 [69, 256, 2048], P(None, 'tensor'), may hold values from -0.046875 to 0.046875
- norm_gain: float32 [2048], replicated, may hold values from 0.1 to 1.9
- attention_in: bfloat16 [2048, 3, 2048], P(None, None, 'tensor'), may hold values from -1 to 1
- attention_out: bfloat16 [2048, 2048], P('tensor'), may hold values from -0.125 to 0.125
Outputs:
- layer_out: bfloat16 [4096, 2048], P(('groups', 'patch', 'tensor')), parts along dimension 0
The draws below stay inside these ranges and needn't reach their ends.
There are 2 independent parts, one for each index of `groups`. The reference program is written for one: setup_inputs(seed, part) draws one part's arguments, and reference() takes and returns one part's arrays. A program takes and returns all parts, laid end to end along the dimension named above; an argument that names none is the same for every part. Nothing has to cross between parts.
Inputs may be any that keep to these rules, and one draw needn't show every extreme that they name: send_index[q, r, s] is a block of sender q's own 256 source blocks. A device names at most 2 slots of one sender in its intersection entries, and exactly 2 of at least one sender; every slot q * 2 + s that a device names is filled by sender q.
All inputs are finite; a program needn't handle non-finite values.
Results may differ from the reference program's by a relative error of at most 0.0085.
Values may be sent and summed in bfloat16 or wider, within the bound.
A program may use at most 192 MiB of HBM per device.

```python
import math
import jax
import jax.numpy as jnp
from jax import lax

C = 69
D = 2048
HEADS = 16
PATCH_PIX = 256
RB = 128
K_OVL = 2
CAP = 2
HD = 128
TOKENS = 2048
NDEV = 16
TB_DEV = 256
SB_DEV = 256
NTB = 4096
NSB = 4096
PB = 128


def plan_counts(key):
    key_raw = jax.random.fold_in(key, 101)
    key_shift = jax.random.fold_in(key, 102)
    raw_counts = jax.random.randint(key_raw, (NDEV, NDEV), 0, CAP + 1)
    offset = jax.random.randint(key_shift, (), 0, NDEV)
    forced = (jnp.arange(NDEV, dtype=jnp.int32) + offset) % NDEV
    is_forced = jnp.arange(NDEV, dtype=jnp.int32)[None, :] == forced[:, None]
    others = jnp.where(is_forced, 0, raw_counts)
    budget = TB_DEV * K_OVL - CAP
    before = jnp.cumsum(others, axis=1) - others
    kept = jnp.minimum(others, jnp.maximum(budget - before, 0))
    return jnp.where(is_forced, CAP, kept)


def draw_send_index(key, part):
    key = jax.random.fold_in(key, 7)
    values = jax.random.randint(key, (NDEV * NDEV * CAP,), 0, SB_DEV)
    position = jnp.arange(NDEV * NDEV * CAP, dtype=jnp.int32)
    values = jnp.where(position == 0, SB_DEV - 1, values)
    values = jnp.where(position == 1, 0, values)
    return values.reshape(NDEV, NDEV, CAP).astype(jnp.int32)


def draw_intersection(key, part):
    key = jax.random.fold_in(key, 11)
    counts = plan_counts(jax.random.fold_in(key, 1))
    slots_all = NDEV * CAP
    position = jnp.arange(slots_all, dtype=jnp.int32)
    peer_of = position // CAP
    slot_of = position % CAP
    used = slot_of[None, :] < counts[:, peer_of]
    used_count = jnp.sum(used.astype(jnp.int32), axis=1)
    ordered = jnp.argsort(jnp.where(used, 0, 1) * slots_all + position[None, :], axis=1).astype(jnp.int32)
    refs_dev = TB_DEV * K_OVL
    ref_pos = jnp.arange(refs_dev, dtype=jnp.int32)
    extra = jax.random.randint(jax.random.fold_in(key, 2), (NDEV, refs_dev), 0, 1 << 20) % used_count[:, None]
    which = jnp.where(ref_pos[None, :] < used_count[:, None], ref_pos[None, :], extra)
    chosen = jnp.take_along_axis(ordered, which, axis=1)
    shuffle_keys = jax.random.randint(jax.random.fold_in(key, 3), (NDEV, refs_dev), 0, 1 << 19) * refs_dev + ref_pos[None, :]
    shuffle = jnp.argsort(shuffle_keys, axis=1).astype(jnp.int32)
    chosen = jnp.take_along_axis(chosen, shuffle, axis=1)
    return chosen.reshape(NDEV * TB_DEV, K_OVL).astype(jnp.int32)


def draw_attention_in(key, part):
    key = jax.random.fold_in(key, 5)
    key_base = jax.random.fold_in(key, 1)
    base = jax.random.truncated_normal(key_base, -6.0, 6.0, (D, 3, D), jnp.float32) * D ** (-0.5)
    return jnp.clip(base, -1.0, 1.0).astype(jnp.bfloat16)


def block_levels(own_key, extent, shards, least, high):
    loudness, own = 1.0, jax.random.fold_in(own_key, 6)
    for dim, parts in shards:
        draws = jnp.exp(jax.random.uniform(jax.random.fold_in(own, dim), (parts,), jnp.float32, least / len(shards), high / len(shards)))
        loudness = loudness * jnp.repeat(draws, extent[dim] // parts).reshape([-1 if axis == dim else 1 for axis in range(len(extent))])
    return loudness


def centred(rng, dims, width, bound, split=(), kind=jnp.bfloat16):
    entries = jax.random.normal(rng, dims, jnp.float32) * width
    if len(split) > 0:
        entries = block_levels(rng, dims, split, -0.22, 0.18) * entries
    return jnp.clip(entries, min=-bound, max=bound).astype(kind)


def setup_inputs(seed: int = 0, part: int = 0) -> dict:
    splits = jax.random.split(jax.random.key(seed), 9)
    own_keys = jax.random.split(jax.random.fold_in(splits[8], part), 9)
    return {
        "source": centred(own_keys[0], (NSB, C, RB), 8.0, 48.0, ((0, 16),)),
        "intersection_tiles": jnp.clip(jnp.exp(math.log(1.0) - 6.9083047 * jax.random.uniform(splits[1], (NTB, K_OVL, RB, PB), jnp.float32) ** block_levels(splits[1], (NTB, K_OVL, RB, PB), ((0, 16),), -0.2, 0.2)), 0.0009994507, 1.0).astype(jnp.bfloat16),
        "send_index": draw_send_index(jax.random.fold_in(splits[8], 71), part),
        "intersection": draw_intersection(jax.random.fold_in(splits[8], 71), part),
        "emb_weight": centred(splits[4], (C, PATCH_PIX, D), (C * PATCH_PIX) ** -0.5, 0.046875, ((1, 4),)),
        "norm_gain": jnp.clip(1.0 + 0.18 * jax.random.normal(splits[5], (D,), jnp.float32), 0.1, 1.9),
        "attention_in": draw_attention_in(jax.random.fold_in(splits[8], 71), part),
        "attention_out": centred(splits[7], (D, D), D ** -0.5, 0.125, ((0, 4),)),
    }


EPS = 1e-05

def regrid_one(source, pieces):
    block_ids, tile_here = pieces
    picked = source[block_ids].astype(jnp.float32)
    weights = tile_here.astype(jnp.float32)
    numer = jnp.einsum('bkcr,bkrp->bcp', picked, weights)
    area = lax.optimization_barrier(jnp.sum(weights, axis=(1, 2)))
    return (numer / area[:, None, :]).astype(jnp.bfloat16)

def one_head(pieces):
    query_head, key_head, value_head = pieces
    scores = jnp.dot(query_head, key_head.T, preferred_element_type=jnp.float32)
    highest = lax.optimization_barrier(jnp.max(scores, axis=-1, keepdims=True))
    expo = jnp.exp(scores - highest)
    denom = lax.optimization_barrier(jnp.sum(expo, axis=-1, keepdims=True))
    weights = expo.astype(jnp.bfloat16)
    summed = jnp.dot(weights, value_head, preferred_element_type=jnp.float32)
    return (summed / denom).astype(jnp.bfloat16)

def reference(source, intersection_tiles, send_index, intersection, emb_weight, norm_gain, attention_in, attention_out):
    receiver = jnp.arange(NDEV * TB_DEV, dtype=jnp.int32) // TB_DEV
    sender = intersection // CAP
    slot_of = intersection % CAP
    local_block = send_index[sender, receiver[:, None], slot_of]
    source_ids = (sender * SB_DEV + local_block).astype(jnp.int32)
    regridded = lax.map(lambda pieces: regrid_one(source, pieces), (source_ids.reshape(NDEV, TB_DEV, K_OVL), intersection_tiles.reshape(NDEV, TB_DEV, K_OVL, RB, PB))).reshape(TOKENS, 2, C, PB)
    pixels = jnp.transpose(regridded, (0, 2, 1, 3)).reshape(TOKENS, C, PATCH_PIX)
    embedded = jnp.einsum('tcx,cxd->td', pixels.astype(jnp.float32), emb_weight.astype(jnp.float32)).astype(jnp.bfloat16)
    features = embedded.astype(jnp.float32)
    scale_rows = lax.rsqrt(lax.optimization_barrier(jnp.mean(features * features, axis=-1, keepdims=True)) + EPS)
    normed = (features * scale_rows * norm_gain.astype(jnp.float32)).astype(jnp.bfloat16)
    proj = jnp.dot(normed, attention_in.reshape(D, 3 * D), preferred_element_type=jnp.float32)
    proj = proj.reshape(TOKENS, 3, HEADS, HD)
    query = (proj[:, 0] * HD ** (-0.5)).astype(jnp.bfloat16)
    keys = proj[:, 1].astype(jnp.bfloat16)
    values = proj[:, 2].astype(jnp.bfloat16)
    heads_out = lax.map(one_head, (jnp.transpose(query, (1, 0, 2)), jnp.transpose(keys, (1, 0, 2)), jnp.transpose(values, (1, 0, 2))))
    heads_out = jnp.transpose(heads_out, (1, 0, 2)).reshape(TOKENS, D)
    mixing = jnp.dot(heads_out, attention_out, preferred_element_type=jnp.float32)
    return (features + mixing).astype(jnp.bfloat16)
```

```python
import functools

import jax
import jax.numpy as jnp
from jax import lax
from jax.experimental import pallas as pl
from jax.experimental.pallas import tpu as pltpu
from jax.sharding import PartitionSpec as P

HD = 128
EPS = 1e-05
LANES = 128
MIB = 1 << 20


def round_up(value, unit):
    return -(-value // unit) * unit


def regrid_kernel(channels, toks, slot_ref, arrived_ref, tiles_ref, out_ref, ordered, stage):
    pairs = (channels + 1) // 2
    half = round_up(pairs + 1, 8)
    step = pl.program_id(0)

    @pl.when(step == 0)
    def _():
        row = lax.broadcasted_iota(jnp.int32, (2 * half, channels), 0)
        col = lax.broadcasted_iota(jnp.int32, (2 * half, channels), 1)
        wanted = jnp.where(row < half, 2 * row, 2 * (row - half) + 1)
        order = jnp.where(wanted == col, 1.0, 0.0).astype(jnp.bfloat16)
        ones = lax.broadcasted_iota(jnp.int32, (2 * half, LANES), 0) == pairs

        @pl.loop(0, arrived_ref.shape[0])
        def _(slot):
            moved = jnp.dot(order, arrived_ref[slot], preferred_element_type=jnp.float32)
            keep = lax.broadcasted_iota(jnp.int32, (2 * half, LANES), 0)
            valid = ((keep < pairs) | ((keep >= half) & (keep < half + channels // 2)))
            moved = jnp.where(valid, moved, 0.0)
            ordered[slot] = jnp.where(ones, 1.0, moved).astype(jnp.bfloat16)

    low = lax.broadcasted_iota(jnp.int32, (half, LANES), 1) < LANES // 2
    for tok in range(toks):
        for side in range(2):
            block = tok * 2 + side
            base = (step * toks * 2 + block) * 2
            lhs = jnp.concatenate([ordered[slot_ref[base]], ordered[slot_ref[base + 1]]], axis=1)
            rhs = tiles_ref[block].reshape(2 * tiles_ref.shape[2], LANES)
            numer = jnp.dot(lhs, rhs, preferred_element_type=jnp.float32)
            area = numer[pairs : pairs + 1]
            value = numer / area
            even, odd = value[:half], value[half:]
            first = jnp.where(low, even, pltpu.roll(odd, LANES // 2, 1))
            second = jnp.where(low, pltpu.roll(even, LANES // 2, 1), odd)
            start = 2 * side * pairs * toks + tok
            stage[pl.ds(start, pairs, stride=toks), :] = first[:pairs]
            stage[pl.ds(start + pairs * toks, pairs, stride=toks), :] = second[:pairs]
    out_ref[...] = stage[...].reshape(4, pairs, toks, LANES).astype(jnp.bfloat16)


def regrid(arrived, tiles, slots, toks=16):
    n_slots, channels, cells = arrived.shape
    blocks = tiles.shape[0]
    tok_local = blocks // 2
    pairs = (channels + 1) // 2
    half = round_up(pairs + 1, 8)
    return pl.pallas_call(
        functools.partial(regrid_kernel, channels, toks),
        out_shape=jax.ShapeDtypeStruct((4, pairs, tok_local, LANES), jnp.bfloat16),
        grid_spec=pltpu.PrefetchScalarGridSpec(
            num_scalar_prefetch=1,
            grid=(tok_local // toks,),
            in_specs=[
                pl.BlockSpec((n_slots, channels, cells), lambda i, s: (0, 0, 0)),
                pl.BlockSpec((2 * toks,) + tiles.shape[1:], lambda i, s: (i, 0, 0, 0)),
            ],
            out_specs=pl.BlockSpec((4, pairs, toks, LANES), lambda i, s: (0, 0, i, 0)),
            scratch_shapes=[
                pltpu.VMEM((n_slots, 2 * half, cells), jnp.bfloat16),
                pltpu.VMEM((4 * pairs * toks, LANES), jnp.float32),
            ],
        ),
        compiler_params=pltpu.CompilerParams(vmem_limit_bytes=40 * MIB),
        name="regrid",
    )(slots, arrived, tiles)


def embed_kernel(pairs, per, channels, px_ref, w_ref, out_ref, lhs, acc):
    step = pl.program_id(0)
    last = pl.num_programs(0) - 1
    senders, _, toks, _ = px_ref.shape
    width = out_ref.shape[1]
    tile = 512

    @pl.when(step == 0)
    def _():
        acc[...] = jnp.zeros_like(acc)

    def multiply(count, rows):
        for s in range(senders):
            for j in range(count):
                lhs[s * toks : (s + 1) * toks, j * LANES : (j + 1) * LANES] = px_ref[s, j]

        @pl.loop(0, width // tile)
        def _(i):
            cols = pl.ds(pl.multiple_of(i * tile, tile), tile)
            w = w_ref[: 2 * count, :, cols].reshape(count * LANES, tile)
            if rows < count * LANES:
                place = lax.broadcasted_iota(jnp.int32, w.shape, 0)
                w = jnp.where(place < rows, w, jnp.zeros_like(w))
            acc[:, cols] += jnp.dot(
                lhs[:, : count * LANES], w, preferred_element_type=jnp.float32
            )

    @pl.when(step < last)
    def _():
        multiply(per, per * LANES)

    @pl.when(step == last)
    def _():
        before = (pairs - 1) // per * per
        multiply(pairs - before, (channels - 2 * before) * (LANES // 2))
        out_ref[...] = acc[...].astype(out_ref.dtype)


def embed(pixels, weight, per=6):
    senders, pairs, toks, _ = pixels.shape
    channels, sub_pix, width = weight.shape
    return pl.pallas_call(
        functools.partial(embed_kernel, pairs, per, channels),
        out_shape=jax.ShapeDtypeStruct((senders * toks, width), jnp.bfloat16),
        grid=(pl.cdiv(pairs, per),),
        in_specs=[
            pl.BlockSpec((senders, per, toks, LANES), lambda i: (0, i, 0, 0)),
            pl.BlockSpec((2 * per, sub_pix, width), lambda i: (i, 0, 0)),
        ],
        out_specs=pl.BlockSpec((senders * toks, width), lambda i: (0, 0)),
        scratch_shapes=[
            pltpu.VMEM((senders * toks, per * LANES), jnp.bfloat16),
            pltpu.VMEM((senders * toks, width), jnp.float32),
        ],
        compiler_params=pltpu.CompilerParams(vmem_limit_bytes=48 * MIB),
        name="embed",
    )(pixels, weight)


def attend_kernel(q_ref, k_ref, v_ref, out_ref):
    scores = lax.dot_general(
        q_ref[...], k_ref[...], (((1,), (1,)), ((), ())), preferred_element_type=jnp.float32
    )
    highest = jnp.max(scores, axis=-1, keepdims=True)
    expo = jnp.exp(scores - highest)
    denom = jnp.sum(expo, axis=-1, keepdims=True)
    summed = jnp.dot(expo.astype(jnp.bfloat16), v_ref[...], preferred_element_type=jnp.float32)
    out_ref[...] = (summed / denom).astype(jnp.bfloat16)


def attend(query, keys, values, rows=256):
    tokens, width = query.shape
    all_tokens = keys.shape[0]
    return pl.pallas_call(
        attend_kernel,
        out_shape=jax.ShapeDtypeStruct(query.shape, jnp.bfloat16),
        grid=(width // HD, tokens // rows),
        in_specs=[
            pl.BlockSpec((rows, HD), lambda h, i: (i, h)),
            pl.BlockSpec((all_tokens, HD), lambda h, i: (0, h)),
            pl.BlockSpec((all_tokens, HD), lambda h, i: (0, h)),
        ],
        out_specs=pl.BlockSpec((rows, HD), lambda h, i: (i, h)),
        compiler_params=pltpu.CompilerParams(vmem_limit_bytes=48 * MIB),
        name="attend",
    )(query, keys, values)


def general_embed(arrived, intersection_tiles, intersection, emb_weight, n_tensor):
    targets, depth, tile_rows, pix_block = intersection_tiles.shape
    _, channels, cell_rows = arrived.shape
    picked = jnp.take(arrived, intersection.reshape(-1), axis=0)
    tok_local = targets // 2
    half_tensor = n_tensor // 2
    sub_pix = pix_block // half_tensor
    picked = picked.reshape(tok_local, 2, depth, channels, cell_rows)
    tile_view = intersection_tiles.reshape(tok_local, 2, depth, tile_rows, half_tensor, sub_pix)
    numer = jnp.einsum("thkcr,thkrap->hactp", picked, tile_view, preferred_element_type=jnp.float32)
    area = jnp.sum(tile_view, axis=(2, 3), dtype=jnp.float32)
    area = jnp.transpose(area, (1, 2, 0, 3))[:, :, None]
    regridded = (numer / area).astype(jnp.bfloat16).reshape(n_tensor, channels, tok_local * sub_pix)
    moved = lax.all_to_all(regridded, "tensor", split_axis=0, concat_axis=2, tiled=True)
    pixels = moved.reshape(channels, n_tensor * tok_local, sub_pix)
    return jnp.einsum(
        "ctq,cqd->td", pixels, emb_weight, preferred_element_type=jnp.float32
    ).astype(jnp.bfloat16)


def on_device(
    source,
    intersection_tiles,
    send_index,
    intersection,
    emb_weight,
    norm_gain,
    attention_in,
    attention_out,
):
    n_tensor = lax.axis_size("tensor")
    blocks_here, channels, cell_rows = source.shape
    peers = send_index.shape[1]
    slots = send_index.shape[2]
    payload = jnp.take(source, send_index.reshape(-1), axis=0, mode="clip").reshape(
        peers, slots, channels, cell_rows
    )
    arrived = lax.all_to_all(payload, ("patch", "tensor"), split_axis=0, concat_axis=0, tiled=True)
    arrived = arrived.reshape(peers * slots, channels, cell_rows)
    if 2 * emb_weight.shape[1] == LANES and intersection_tiles.shape[0] % 32 == 0:
        pixels = regrid(arrived, intersection_tiles, intersection.reshape(-1))
        pixels = lax.all_to_all(pixels, "tensor", split_axis=0, concat_axis=0, tiled=True)
        partial = embed(pixels, emb_weight)
    else:
        partial = general_embed(arrived, intersection_tiles, intersection, emb_weight, n_tensor)
    own_rows = lax.psum_scatter(partial, "tensor", scatter_dimension=0, tiled=True)
    values_f = own_rows.astype(jnp.float32)
    factor = lax.rsqrt(jnp.mean(values_f * values_f, axis=-1, keepdims=True) + EPS)
    normed = (values_f * factor * norm_gain).astype(jnp.bfloat16)
    normed = lax.all_gather(normed, "tensor", axis=0, tiled=True)

    def project(part):
        return jnp.dot(normed, attention_in[:, part], preferred_element_type=jnp.float32)

    keys = lax.all_gather(project(1).astype(jnp.bfloat16), "patch", axis=0, tiled=True)
    values = lax.all_gather(project(2).astype(jnp.bfloat16), "patch", axis=0, tiled=True)
    query = (project(0) * HD ** (-0.5)).astype(jnp.bfloat16)
    heads_out = attend(query, keys, values)
    mixing = lax.psum_scatter(
        jnp.dot(heads_out, attention_out, preferred_element_type=jnp.float32).astype(jnp.bfloat16),
        "tensor",
        scatter_dimension=0,
        tiled=True,
    ).astype(jnp.float32)
    return (values_f + mixing).astype(jnp.bfloat16)


def solution(mesh):
    placed = (
        P(("groups", "patch", "tensor"), None, None),
        P(("patch", "tensor"), None, None, None),
        P(("patch", "tensor"), None, None),
        P(("patch", "tensor"), None),
        P(None, "tensor", None),
        P(),
        P(None, None, "tensor"),
        P("tensor", None),
    )
    return jax.shard_map(
        on_device,
        mesh=mesh,
        in_specs=placed,
        out_specs=P(("groups", "patch", "tensor"), None),
        check_vma=False,
    )
```

```python
import functools

import jax
import jax.numpy as jnp
from jax import lax
from jax.experimental import pallas as pl
from jax.experimental.pallas import tpu as pltpu
from jax.sharding import PartitionSpec as P

HD = 128
EPS = 1e-05
LANES = 128
MIB = 1 << 20


def round_up(value, unit):
    return -(-value // unit) * unit


def regrid_kernel(channels, toks, slot_ref, arrived_ref, tiles_ref, out_ref, ordered, stage):
    pairs = (channels + 1) // 2
    half = round_up(pairs + 1, 8)
    step = pl.program_id(0)

    @pl.when(step == 0)
    def _():
        row = lax.broadcasted_iota(jnp.int32, (2 * half, channels), 0)
        col = lax.broadcasted_iota(jnp.int32, (2 * half, channels), 1)
        wanted = jnp.where(row < half, 2 * row, 2 * (row - half) + 1)
        order = jnp.where(wanted == col, 1.0, 0.0).astype(jnp.bfloat16)
        ones = lax.broadcasted_iota(jnp.int32, (2 * half, LANES), 0) == pairs

        @pl.loop(0, arrived_ref.shape[0])
        def _(slot):
            moved = jnp.dot(order, arrived_ref[slot], preferred_element_type=jnp.float32)
            keep = lax.broadcasted_iota(jnp.int32, (2 * half, LANES), 0)
            valid = ((keep < pairs) | ((keep >= half) & (keep < half + channels // 2)))
            moved = jnp.where(valid, moved, 0.0)
            ordered[slot] = jnp.where(ones, 1.0, moved).astype(jnp.bfloat16)

    low = lax.broadcasted_iota(jnp.int32, (half, LANES), 1) < LANES // 2
    for tok in range(toks):
        for side in range(2):
            block = tok * 2 + side
            base = (step * toks * 2 + block) * 2
            lhs = jnp.concatenate([ordered[slot_ref[base]], ordered[slot_ref[base + 1]]], axis=1)
            rhs = tiles_ref[block].reshape(2 * tiles_ref.shape[2], LANES)
            numer = jnp.dot(lhs, rhs, preferred_element_type=jnp.float32)
            area = numer[pairs : pairs + 1]
            value = numer / area
            even, odd = value[:half], value[half:]
            first = jnp.where(low, even, pltpu.roll(odd, LANES // 2, 1))
            second = jnp.where(low, pltpu.roll(even, LANES // 2, 1), odd)
            start = 2 * side * pairs * toks + tok
            stage[pl.ds(start, pairs, stride=toks), :] = first[:pairs]
            stage[pl.ds(start + pairs * toks, pairs, stride=toks), :] = second[:pairs]
    out_ref[...] = stage[...].reshape(4, pairs, toks, LANES).astype(jnp.bfloat16)


def regrid(arrived, tiles, slots, toks=16):
    n_slots, channels, cells = arrived.shape
    blocks = tiles.shape[0]
    tok_local = blocks // 2
    pairs = (channels + 1) // 2
    half = round_up(pairs + 1, 8)
    return pl.pallas_call(
        functools.partial(regrid_kernel, channels, toks),
        out_shape=jax.ShapeDtypeStruct((4, pairs, tok_local, LANES), jnp.bfloat16),
        grid_spec=pltpu.PrefetchScalarGridSpec(
            num_scalar_prefetch=1,
            grid=(tok_local // toks,),
            in_specs=[
                pl.BlockSpec((n_slots, channels, cells), lambda i, s: (0, 0, 0)),
                pl.BlockSpec((2 * toks,) + tiles.shape[1:], lambda i, s: (i, 0, 0, 0)),
            ],
            out_specs=pl.BlockSpec((4, pairs, toks, LANES), lambda i, s: (0, 0, i, 0)),
            scratch_shapes=[
                pltpu.VMEM((n_slots, 2 * half, cells), jnp.bfloat16),
                pltpu.VMEM((4 * pairs * toks, LANES), jnp.float32),
            ],
        ),
        compiler_params=pltpu.CompilerParams(vmem_limit_bytes=40 * MIB),
        name="regrid",
    )(slots, arrived, tiles)


def peer_of(axis, far):
    me = lax.axis_index(axis)
    if far == 1:
        return me + 1 - 2 * lax.rem(me, 2)
    if far == 2:
        return lax.rem(me + 2, 4)
    return 3 - me


def greet(pairs_of):
    barrier = pltpu.get_barrier_semaphore()
    for axis, far in pairs_of:
        pl.semaphore_signal(
            barrier,
            inc=1,
            device_id={axis: peer_of(axis, far)},
            device_id_type=pl.DeviceIdType.MESH,
        )
    pl.semaphore_wait(barrier, len(pairs_of))


def push(src, dst, send, recv, axis, far):
    return pltpu.make_async_remote_copy(
        src_ref=src,
        dst_ref=dst,
        send_sem=send,
        recv_sem=recv,
        device_id={axis: peer_of(axis, far)},
        device_id_type=pl.DeviceIdType.MESH,
    )


def embed_kernel(
    channels,
    px_ref,
    w_ref,
    out_ref,
    recv,
    w,
    lhs,
    part,
    got,
    total,
    local_sem,
    send_sem,
    recv_sem,
    part_send,
    part_recv,
):
    _, pairs, toks, _ = recv.shape
    tiles, _, tile = total.shape
    me = lax.axis_index("tensor")
    load = pltpu.make_async_copy(w_ref, w.at[pl.ds(0, channels)], local_sem.at[0])
    load.start()
    own = pltpu.make_async_copy(px_ref.at[me], recv.at[0], local_sem.at[1])
    own.start()
    if channels < 2 * pairs:
        w[channels:] = jnp.zeros((2 * pairs - channels,) + w.shape[1:], w.dtype)
    greet([("tensor", far) for far in (1, 2, 3)])
    moves = [
        push(
            px_ref.at[peer_of("tensor", far)],
            recv.at[far],
            send_sem.at[far - 1],
            recv_sem.at[far - 1],
            "tensor",
            far,
        )
        for far in (1, 2, 3)
    ]
    moves[1].start()
    moves[0].start()

    def back(far, i):
        return push(
            part.at[far - 1, i],
            got.at[far - 1, i],
            part_send.at[far - 1, i],
            part_recv.at[far - 1, i],
            "tensor",
            far,
        )

    def multiply(far):
        @pl.loop(0, pairs)
        def _(j):
            lhs[:, pl.ds(pl.multiple_of(j * LANES, LANES), LANES)] = recv[far, j]

        @pl.loop(0, tiles)
        def _(i):
            cols = pl.ds(pl.multiple_of(i * tile, tile), tile)
            rhs = w[:, :, cols].reshape(pairs * LANES, tile)
            summed = jnp.dot(lhs[...], rhs, preferred_element_type=jnp.float32)
            if far == 0:
                total[i] = summed
            else:
                part[far - 1, i] = summed.astype(part.dtype)
                back(far, i).start()

    own.wait()
    load.wait()
    multiply(0)
    moves[1].wait_send()
    moves[2].start()
    moves[1].wait_recv()
    multiply(2)
    moves[0].wait()
    multiply(1)
    moves[2].wait()
    multiply(3)

    @pl.loop(0, tiles)
    def _(i):
        summed = total[i]
        for far in (1, 2, 3):
            back(far, i).wait()
            summed += got[far - 1, i].astype(jnp.float32)
        cols = pl.ds(pl.multiple_of(i * tile, tile), tile)
        out_ref[:, cols] = summed.astype(out_ref.dtype)


def embed(pixels, weight, tile=512):
    senders, pairs, toks, _ = pixels.shape
    channels, sub_pix, width = weight.shape
    tiles = width // tile
    return pl.pallas_call(
        functools.partial(embed_kernel, channels),
        out_shape=jax.ShapeDtypeStruct((toks, width), jnp.bfloat16),
        in_specs=[pl.BlockSpec(memory_space=pl.ANY)] * 2,
        out_specs=pl.BlockSpec(memory_space=pltpu.VMEM),
        scratch_shapes=[
            pltpu.VMEM(pixels.shape, jnp.bfloat16),
            pltpu.VMEM((2 * pairs, sub_pix, width), jnp.bfloat16),
            pltpu.VMEM((toks, pairs * LANES), jnp.bfloat16),
            pltpu.VMEM((3, tiles, toks, tile), jnp.bfloat16),
            pltpu.VMEM((3, tiles, toks, tile), jnp.bfloat16),
            pltpu.VMEM((tiles, toks, tile), jnp.float32),
            pltpu.SemaphoreType.DMA((2,)),
            pltpu.SemaphoreType.DMA((3,)),
            pltpu.SemaphoreType.DMA((3,)),
            pltpu.SemaphoreType.DMA((3, tiles)),
            pltpu.SemaphoreType.DMA((3, tiles)),
        ],
        compiler_params=pltpu.CompilerParams(
            collective_id=0, has_side_effects=True, vmem_limit_bytes=50 * MIB
        ),
        name="embed",
    )(pixels, weight)


def project_kernel(
    x_ref,
    gain_ref,
    w_ref,
    q_ref,
    k_ref,
    v_ref,
    rows,
    w,
    load_sem,
    row_send,
    row_recv,
    key_send,
    key_recv,
    value_send,
    value_recv,
):
    load = pltpu.make_async_copy(w_ref, w, load_sem)
    load.start()
    values = x_ref[...].astype(jnp.float32)
    factor = lax.rsqrt(jnp.mean(values * values, axis=-1, keepdims=True) + EPS)
    rows[0] = (values * factor * gain_ref[...]).astype(jnp.bfloat16)
    toks = rows.shape[1]
    greet([("tensor", 1), ("tensor", 2), ("patch", 1), ("patch", 2)])

    def row_move(src, dst, far):
        return push(rows.at[src], rows.at[dst], row_send.at[dst], row_recv.at[dst], "tensor", far)

    across = row_move(0, 2, 2)
    beside = row_move(0, 1, 1)
    relay = row_move(2, 3, 1)
    across.start()
    beside.start()
    load.wait()

    def cross(block, src, dst, far):
        return [
            push(
                ref.at[src, block],
                ref.at[dst, block],
                sent.at[dst, block],
                came.at[dst, block],
                "patch",
                far,
            )
            for ref, sent, came in (
                (k_ref, key_send, key_recv),
                (v_ref, value_send, value_recv),
            )
        ]

    def project(block):
        x = rows[block]
        k_ref[0, block] = jnp.dot(x, w[1], preferred_element_type=jnp.float32).astype(jnp.bfloat16)
        v_ref[0, block] = jnp.dot(x, w[2], preferred_element_type=jnp.float32).astype(jnp.bfloat16)
        for copy in cross(block, 0, 2, 2) + cross(block, 0, 1, 1):
            copy.start()
        query = jnp.dot(x, w[0], preferred_element_type=jnp.float32) * HD ** (-0.5)
        place = lax.axis_index("tensor") if block == 0 else peer_of("tensor", block)
        q_ref[pl.ds(pl.multiple_of(place * toks, toks), toks), :] = query.astype(jnp.bfloat16)

    project(0)
    across.wait_recv()
    relay.start()
    project(2)
    beside.wait_recv()
    project(1)
    for block in (0, 2):
        for copy in cross(block, 0, 2, 2):
            copy.wait_recv()
        for copy in cross(block, 2, 3, 1):
            copy.start()
    relay.wait_recv()
    project(3)
    for block in (1, 3):
        for copy in cross(block, 0, 2, 2):
            copy.wait_recv()
        for copy in cross(block, 2, 3, 1):
            copy.start()
    for block in range(4):
        for copy in cross(block, 0, 1, 1) + cross(block, 2, 3, 1):
            copy.wait()
        for copy in cross(block, 0, 2, 2):
            copy.wait_send()
    for copy in (across, beside, relay):
        copy.wait_send()


def project_all(x, gain, weight):
    toks, width = x.shape
    heads_width = weight.shape[2]
    kept = jax.ShapeDtypeStruct((4, 4, toks, heads_width), jnp.bfloat16)
    in_vmem = pl.BlockSpec(memory_space=pltpu.VMEM)
    query, keys, values = pl.pallas_call(
        project_kernel,
        out_shape=(jax.ShapeDtypeStruct((4 * toks, heads_width), jnp.bfloat16), kept, kept),
        in_specs=[in_vmem, in_vmem, pl.BlockSpec(memory_space=pl.ANY)],
        out_specs=(in_vmem, in_vmem, in_vmem),
        scratch_shapes=[
            pltpu.VMEM((4, toks, width), jnp.bfloat16),
            pltpu.VMEM(weight.shape, jnp.bfloat16),
            pltpu.SemaphoreType.DMA,
            pltpu.SemaphoreType.DMA((4,)),
            pltpu.SemaphoreType.DMA((4,)),
        ]
        + [pltpu.SemaphoreType.DMA((4, 4))] * 4,
        compiler_params=pltpu.CompilerParams(
            collective_id=1, has_side_effects=True, vmem_limit_bytes=40 * MIB
        ),
        name="project_all",
    )(x, gain, weight)
    return query, keys.reshape(-1, heads_width), values.reshape(-1, heads_width)


def attend_kernel(q_ref, k_ref, v_ref, out_ref):
    scores = lax.dot_general(
        q_ref[...], k_ref[...], (((1,), (1,)), ((), ())), preferred_element_type=jnp.float32
    )
    highest = jnp.max(scores, axis=-1, keepdims=True)
    expo = jnp.exp(scores - highest)
    denom = jnp.sum(expo, axis=-1, keepdims=True)
    summed = jnp.dot(expo.astype(jnp.bfloat16), v_ref[...], preferred_element_type=jnp.float32)
    out_ref[...] = (summed / denom).astype(jnp.bfloat16)


def attend(query, keys, values, rows=256):
    tokens, width = query.shape
    all_tokens = keys.shape[0]
    return pl.pallas_call(
        attend_kernel,
        out_shape=jax.ShapeDtypeStruct(query.shape, jnp.bfloat16),
        grid=(width // HD, tokens // rows),
        in_specs=[
            pl.BlockSpec((rows, HD), lambda h, i: (i, h)),
            pl.BlockSpec((all_tokens, HD), lambda h, i: (0, h)),
            pl.BlockSpec((all_tokens, HD), lambda h, i: (0, h)),
        ],
        out_specs=pl.BlockSpec((rows, HD), lambda h, i: (i, h)),
        compiler_params=pltpu.CompilerParams(vmem_limit_bytes=48 * MIB),
        name="attend",
    )(query, keys, values)


def general_embed(arrived, intersection_tiles, intersection, emb_weight, n_tensor):
    targets, depth, tile_rows, pix_block = intersection_tiles.shape
    _, channels, cell_rows = arrived.shape
    picked = jnp.take(arrived, intersection.reshape(-1), axis=0)
    tok_local = targets // 2
    half_tensor = n_tensor // 2
    sub_pix = pix_block // half_tensor
    picked = picked.reshape(tok_local, 2, depth, channels, cell_rows)
    tile_view = intersection_tiles.reshape(tok_local, 2, depth, tile_rows, half_tensor, sub_pix)
    numer = jnp.einsum("thkcr,thkrap->hactp", picked, tile_view, preferred_element_type=jnp.float32)
    area = jnp.sum(tile_view, axis=(2, 3), dtype=jnp.float32)
    area = jnp.transpose(area, (1, 2, 0, 3))[:, :, None]
    regridded = (numer / area).astype(jnp.bfloat16).reshape(n_tensor, channels, tok_local * sub_pix)
    moved = lax.all_to_all(regridded, "tensor", split_axis=0, concat_axis=2, tiled=True)
    pixels = moved.reshape(channels, n_tensor * tok_local, sub_pix)
    return jnp.einsum(
        "ctq,cqd->td", pixels, emb_weight, preferred_element_type=jnp.float32
    ).astype(jnp.bfloat16)


def general_project(own_rows, norm_gain, attention_in):
    values_f = own_rows.astype(jnp.float32)
    factor = lax.rsqrt(jnp.mean(values_f * values_f, axis=-1, keepdims=True) + EPS)
    normed = (values_f * factor * norm_gain).astype(jnp.bfloat16)
    normed = lax.all_gather(normed, "tensor", axis=0, tiled=True)

    def project(part):
        return jnp.dot(normed, attention_in[:, part], preferred_element_type=jnp.float32)

    keys = lax.all_gather(project(1).astype(jnp.bfloat16), "patch", axis=0, tiled=True)
    values = lax.all_gather(project(2).astype(jnp.bfloat16), "patch", axis=0, tiled=True)
    return (project(0) * HD ** (-0.5)).astype(jnp.bfloat16), keys, values


def on_device(
    source,
    intersection_tiles,
    send_index,
    intersection,
    emb_weight,
    norm_gain,
    attention_in,
    attention_out,
):
    n_tensor = lax.axis_size("tensor")
    blocks_here, channels, cell_rows = source.shape
    peers = send_index.shape[1]
    slots = send_index.shape[2]
    payload = jnp.take(source, send_index.reshape(-1), axis=0, mode="clip").reshape(
        peers, slots, channels, cell_rows
    )
    arrived = lax.all_to_all(payload, ("patch", "tensor"), split_axis=0, concat_axis=0, tiled=True)
    arrived = arrived.reshape(peers * slots, channels, cell_rows)
    if (
        2 * emb_weight.shape[1] == LANES
        and n_tensor == 4
        and lax.axis_size("patch") == 4
        and intersection_tiles.shape[0] % 32 == 0
    ):
        pixels = regrid(arrived, intersection_tiles, intersection.reshape(-1))
        own_rows = embed(pixels, emb_weight)
        query, keys, values = project_all(
            own_rows, norm_gain[None, :], jnp.transpose(attention_in, (1, 0, 2))
        )
    else:
        partial = general_embed(arrived, intersection_tiles, intersection, emb_weight, n_tensor)
        own_rows = lax.psum_scatter(partial, "tensor", scatter_dimension=0, tiled=True)
        query, keys, values = general_project(own_rows, norm_gain, attention_in)
    heads_out = attend(query, keys, values)
    mixing = lax.psum_scatter(
        jnp.dot(heads_out, attention_out, preferred_element_type=jnp.float32).astype(jnp.bfloat16),
        "tensor",
        scatter_dimension=0,
        tiled=True,
    ).astype(jnp.float32)
    return (own_rows.astype(jnp.float32) + mixing).astype(jnp.bfloat16)


def solution(mesh):
    placed = (
        P(("groups", "patch", "tensor"), None, None),
        P(("patch", "tensor"), None, None, None),
        P(("patch", "tensor"), None, None),
        P(("patch", "tensor"), None),
        P(None, "tensor", None),
        P(),
        P(None, None, "tensor"),
        P("tensor", None),
    )
    return jax.shard_map(
        on_device,
        mesh=mesh,
        in_specs=placed,
        out_specs=P(("groups", "patch", "tensor"), None),
        check_vma=False,
    )
```

```python
import functools

import jax
import jax.numpy as jnp
from jax import lax
from jax.experimental import pallas as pl
from jax.experimental.pallas import tpu as pltpu
from jax.sharding import PartitionSpec as P

HD = 128
EPS = 1e-05
LANES = 128
MIB = 1 << 20


def round_up(value, unit):
    return -(-value // unit) * unit


def regrid_kernel(channels, toks, slot_ref, arrived_ref, tiles_ref, out_ref, ordered, stage):
    pairs = (channels + 1) // 2
    half = round_up(pairs + 1, 8)
    step = pl.program_id(0)

    @pl.when(step == 0)
    def _():
        row = lax.broadcasted_iota(jnp.int32, (2 * half, channels), 0)
        col = lax.broadcasted_iota(jnp.int32, (2 * half, channels), 1)
        wanted = jnp.where(row < half, 2 * row, 2 * (row - half) + 1)
        order = jnp.where(wanted == col, 1.0, 0.0).astype(jnp.bfloat16)
        ones = lax.broadcasted_iota(jnp.int32, (2 * half, LANES), 0) == pairs

        @pl.loop(0, arrived_ref.shape[0])
        def _(slot):
            moved = jnp.dot(order, arrived_ref[slot], preferred_element_type=jnp.float32)
            keep = lax.broadcasted_iota(jnp.int32, (2 * half, LANES), 0)
            valid = ((keep < pairs) | ((keep >= half) & (keep < half + channels // 2)))
            moved = jnp.where(valid, moved, 0.0)
            ordered[slot] = jnp.where(ones, 1.0, moved).astype(jnp.bfloat16)

    low = lax.broadcasted_iota(jnp.int32, (half, LANES), 1) < LANES // 2
    for tok in range(toks):
        for side in range(2):
            block = tok * 2 + side
            base = (step * toks * 2 + block) * 2
            lhs = jnp.concatenate([ordered[slot_ref[base]], ordered[slot_ref[base + 1]]], axis=1)
            rhs = tiles_ref[block].reshape(2 * tiles_ref.shape[2], LANES)
            numer = jnp.dot(lhs, rhs, preferred_element_type=jnp.float32)
            area = numer[pairs : pairs + 1]
            value = numer * (1.0 / area)
            even, odd = value[:half], value[half:]
            first = jnp.where(low, even, pltpu.roll(odd, LANES // 2, 1))
            second = jnp.where(low, pltpu.roll(even, LANES // 2, 1), odd)
            start = 2 * side * pairs * toks + tok
            stage[pl.ds(start, pairs, stride=toks), :] = first[:pairs]
            stage[pl.ds(start + pairs * toks, pairs, stride=toks), :] = second[:pairs]
    out_ref[...] = stage[...].reshape(4, pairs, toks, LANES).astype(jnp.bfloat16)


def regrid(arrived, tiles, slots, toks=16):
    n_slots, channels, cells = arrived.shape
    blocks = tiles.shape[0]
    tok_local = blocks // 2
    pairs = (channels + 1) // 2
    half = round_up(pairs + 1, 8)
    return pl.pallas_call(
        functools.partial(regrid_kernel, channels, toks),
        out_shape=jax.ShapeDtypeStruct((4, pairs, tok_local, LANES), jnp.bfloat16),
        grid_spec=pltpu.PrefetchScalarGridSpec(
            num_scalar_prefetch=1,
            grid=(tok_local // toks,),
            in_specs=[
                pl.BlockSpec((n_slots, channels, cells), lambda i, s: (0, 0, 0)),
                pl.BlockSpec((2 * toks,) + tiles.shape[1:], lambda i, s: (i, 0, 0, 0)),
            ],
            out_specs=pl.BlockSpec((4, pairs, toks, LANES), lambda i, s: (0, 0, i, 0)),
            scratch_shapes=[
                pltpu.VMEM((n_slots, 2 * half, cells), jnp.bfloat16),
                pltpu.VMEM((4 * pairs * toks, LANES), jnp.float32),
            ],
        ),
        compiler_params=pltpu.CompilerParams(vmem_limit_bytes=40 * MIB),
        name="regrid",
    )(slots, arrived, tiles)


def peer_of(axis, far):
    me = lax.axis_index(axis)
    if far == 1:
        return me + 1 - 2 * lax.rem(me, 2)
    if far == 2:
        return lax.rem(me + 2, 4)
    return 3 - me


def greet(pairs_of):
    barrier = pltpu.get_barrier_semaphore()
    for axis, far in pairs_of:
        pl.semaphore_signal(
            barrier,
            inc=1,
            device_id={axis: peer_of(axis, far)},
            device_id_type=pl.DeviceIdType.MESH,
        )
    pl.semaphore_wait(barrier, len(pairs_of))


def push(src, dst, send, recv, axis, far):
    return pltpu.make_async_remote_copy(
        src_ref=src,
        dst_ref=dst,
        send_sem=send,
        recv_sem=recv,
        device_id={axis: peer_of(axis, far)},
        device_id_type=pl.DeviceIdType.MESH,
    )


def embed_kernel(
    channels,
    px_ref,
    w_ref,
    out_ref,
    recv,
    w,
    lhs,
    part,
    got,
    total,
    local_sem,
    send_sem,
    recv_sem,
    part_send,
    part_recv,
):
    _, pairs, toks, _ = recv.shape
    tiles, _, tile = total.shape
    me = lax.axis_index("tensor")
    load = pltpu.make_async_copy(w_ref, w.at[pl.ds(0, channels)], local_sem.at[0])
    load.start()
    own = pltpu.make_async_copy(px_ref.at[me], recv.at[0], local_sem.at[1])
    own.start()
    if channels < 2 * pairs:
        w[channels:] = jnp.zeros((2 * pairs - channels,) + w.shape[1:], w.dtype)
    greet([("tensor", far) for far in (1, 2, 3)])
    moves = [
        push(
            px_ref.at[peer_of("tensor", far)],
            recv.at[far],
            send_sem.at[far - 1],
            recv_sem.at[far - 1],
            "tensor",
            far,
        )
        for far in (1, 2, 3)
    ]
    moves[2].start()
    moves[0].start()

    def back(far, i):
        return push(
            part.at[far - 1, i],
            got.at[far - 1, i],
            part_send.at[far - 1, i],
            part_recv.at[far - 1, i],
            "tensor",
            2 if far == 2 else 1,
        )

    def multiply(far):
        @pl.loop(0, pairs)
        def _(j):
            lhs[:, pl.ds(pl.multiple_of(j * LANES, LANES), LANES)] = recv[far, j]

        @pl.loop(0, tiles)
        def _(i):
            cols = pl.ds(pl.multiple_of(i * tile, tile), tile)
            rhs = w[:, :, cols].reshape(pairs * LANES, tile)
            summed = jnp.dot(lhs[...], rhs, preferred_element_type=jnp.float32)
            if far == 0:
                total[i] = summed
            else:
                if far == 2:
                    back(3, i).wait_recv()
                    summed += got[2, i].astype(jnp.float32)
                part[far - 1, i] = summed.astype(part.dtype)
                back(far, i).start()

    own.wait()
    load.wait()
    multiply(0)
    moves[2].wait_send()
    moves[1].start()
    moves[2].wait_recv()
    multiply(3)
    moves[0].wait()
    multiply(1)
    moves[1].wait()
    multiply(2)

    @pl.loop(0, tiles)
    def _(i):
        back(3, i).wait_send()
        summed = total[i]
        for far in (1, 2):
            back(far, i).wait()
            summed += got[far - 1, i].astype(jnp.float32)
        cols = pl.ds(pl.multiple_of(i * tile, tile), tile)
        out_ref[:, cols] = summed.astype(out_ref.dtype)


def embed(pixels, weight, tile=512):
    senders, pairs, toks, _ = pixels.shape
    channels, sub_pix, width = weight.shape
    tiles = width // tile
    return pl.pallas_call(
        functools.partial(embed_kernel, channels),
        out_shape=jax.ShapeDtypeStruct((toks, width), jnp.bfloat16),
        in_specs=[pl.BlockSpec(memory_space=pl.ANY)] * 2,
        out_specs=pl.BlockSpec(memory_space=pltpu.VMEM),
        scratch_shapes=[
            pltpu.VMEM(pixels.shape, jnp.bfloat16),
            pltpu.VMEM((2 * pairs, sub_pix, width), jnp.bfloat16),
            pltpu.VMEM((toks, pairs * LANES), jnp.bfloat16),
            pltpu.VMEM((3, tiles, toks, tile), jnp.bfloat16),
            pltpu.VMEM((3, tiles, toks, tile), jnp.bfloat16),
            pltpu.VMEM((tiles, toks, tile), jnp.float32),
            pltpu.SemaphoreType.DMA((2,)),
            pltpu.SemaphoreType.DMA((3,)),
            pltpu.SemaphoreType.DMA((3,)),
            pltpu.SemaphoreType.DMA((3, tiles)),
            pltpu.SemaphoreType.DMA((3, tiles)),
        ],
        compiler_params=pltpu.CompilerParams(
            collective_id=0, has_side_effects=True, vmem_limit_bytes=50 * MIB
        ),
        name="embed",
    )(pixels, weight)


def project_kernel(
    x_ref,
    gain_ref,
    w_ref,
    q_ref,
    k_ref,
    v_ref,
    rows,
    w,
    load_sem,
    row_send,
    row_recv,
    key_send,
    key_recv,
    value_send,
    value_recv,
):
    load = pltpu.make_async_copy(w_ref, w, load_sem)
    load.start()
    values = x_ref[...].astype(jnp.float32)
    factor = lax.rsqrt(jnp.mean(values * values, axis=-1, keepdims=True) + EPS)
    rows[0] = (values * factor * gain_ref[...]).astype(jnp.bfloat16)
    toks = rows.shape[1]
    greet([("tensor", 1), ("tensor", 2), ("patch", 1), ("patch", 2)])

    def row_move(src, dst, far):
        return push(rows.at[src], rows.at[dst], row_send.at[dst], row_recv.at[dst], "tensor", far)

    across = row_move(0, 2, 2)
    beside = row_move(0, 1, 1)
    relay = row_move(2, 3, 1)
    across.start()
    beside.start()
    load.wait()

    def cross(block, src, dst, far):
        return [
            push(
                ref.at[src, block],
                ref.at[dst, block],
                sent.at[dst, block],
                came.at[dst, block],
                "patch",
                far,
            )
            for ref, sent, came in (
                (k_ref, key_send, key_recv),
                (v_ref, value_send, value_recv),
            )
        ]

    def project(block):
        x = rows[block]
        k_ref[0, block] = jnp.dot(x, w[1], preferred_element_type=jnp.float32).astype(jnp.bfloat16)
        v_ref[0, block] = jnp.dot(x, w[2], preferred_element_type=jnp.float32).astype(jnp.bfloat16)
        for copy in cross(block, 0, 2, 2) + cross(block, 0, 1, 1):
            copy.start()
        query = jnp.dot(x, w[0], preferred_element_type=jnp.float32) * HD ** (-0.5)
        place = lax.axis_index("tensor") if block == 0 else peer_of("tensor", block)
        q_ref[pl.ds(pl.multiple_of(place * toks, toks), toks), :] = query.astype(jnp.bfloat16)

    project(0)
    across.wait_recv()
    relay.start()
    project(2)
    beside.wait_recv()
    project(1)
    for block in (0, 2):
        for copy in cross(block, 0, 2, 2):
            copy.wait_recv()
        for copy in cross(block, 2, 3, 1):
            copy.start()
    relay.wait_recv()
    project(3)
    for block in (1, 3):
        for copy in cross(block, 0, 2, 2):
            copy.wait_recv()
        for copy in cross(block, 2, 3, 1):
            copy.start()
    for block in range(4):
        for copy in cross(block, 0, 1, 1) + cross(block, 2, 3, 1):
            copy.wait()
        for copy in cross(block, 0, 2, 2):
            copy.wait_send()
    for copy in (across, beside, relay):
        copy.wait_send()


def project_all(x, gain, weight):
    toks, width = x.shape
    heads_width = weight.shape[2]
    kept = jax.ShapeDtypeStruct((4, 4, toks, heads_width), jnp.bfloat16)
    in_vmem = pl.BlockSpec(memory_space=pltpu.VMEM)
    query, keys, values = pl.pallas_call(
        project_kernel,
        out_shape=(jax.ShapeDtypeStruct((4 * toks, heads_width), jnp.bfloat16), kept, kept),
        in_specs=[in_vmem, in_vmem, pl.BlockSpec(memory_space=pl.ANY)],
        out_specs=(in_vmem, in_vmem, in_vmem),
        scratch_shapes=[
            pltpu.VMEM((4, toks, width), jnp.bfloat16),
            pltpu.VMEM(weight.shape, jnp.bfloat16),
            pltpu.SemaphoreType.DMA,
            pltpu.SemaphoreType.DMA((4,)),
            pltpu.SemaphoreType.DMA((4,)),
        ]
        + [pltpu.SemaphoreType.DMA((4, 4))] * 4,
        compiler_params=pltpu.CompilerParams(
            collective_id=1, has_side_effects=True, vmem_limit_bytes=40 * MIB
        ),
        name="project_all",
    )(x, gain, weight)
    return query, keys.reshape(-1, heads_width), values.reshape(-1, heads_width)


def attend_rows(query, keys, values):
    scores = lax.dot_general(
        query, keys, (((1,), (1,)), ((), ())), preferred_element_type=jnp.float32
    )
    highest = jnp.max(scores, axis=-1, keepdims=True)
    expo = jnp.exp(scores - highest)
    denom = jnp.sum(expo, axis=-1, keepdims=True)
    summed = jnp.dot(expo.astype(jnp.bfloat16), values, preferred_element_type=jnp.float32)
    return (summed / denom).astype(jnp.bfloat16)


def attend_kernel(q_ref, k_ref, v_ref, out_ref):
    out_ref[...] = attend_rows(q_ref[...], k_ref[...], v_ref[...])


def mix_kernel(
    q_ref, k_ref, v_ref, w_ref, x_ref, out_ref, heads, total, part, got, send_sem, recv_sem
):
    _, tiles, toks, tile = part.shape

    def back(far, i):
        return push(
            part.at[far - 1, i],
            got.at[far - 1, i],
            send_sem.at[far - 1, i],
            recv_sem.at[far - 1, i],
            "tensor",
            2 if far == 2 else 1,
        )

    def attended(far):
        place = lax.axis_index("tensor") if far == 0 else peer_of("tensor", far)
        rows = pl.ds(pl.multiple_of(place * toks, toks), toks)
        for head in range(heads.shape[1] // HD):
            lanes = slice(head * HD, (head + 1) * HD)
            heads[:, lanes] = attend_rows(q_ref[rows, lanes], k_ref[:, lanes], v_ref[:, lanes])

    def mixed(i):
        cols = slice(i * tile, (i + 1) * tile)
        return jnp.dot(heads[...], w_ref[:, cols], preferred_element_type=jnp.float32)

    greet([("tensor", 1), ("tensor", 2)])
    attended(3)
    for i in range(tiles):
        part[2, i] = mixed(i).astype(part.dtype)
        back(3, i).start()
    attended(2)
    for i in range(tiles):
        total[i] = mixed(i)
    attended(1)
    for i in range(tiles):
        part[0, i] = mixed(i).astype(part.dtype)
    for i in range(tiles):
        back(3, i).wait_recv()
        part[1, i] = (total[i] + got[2, i].astype(jnp.float32)).astype(part.dtype)
        back(2, i).start()
        back(1, i).start()
    attended(0)
    for i in range(tiles):
        total[i] = mixed(i)
    for i in range(tiles):
        back(3, i).wait_send()
        back(1, i).wait()
        back(2, i).wait()
        cols = slice(i * tile, (i + 1) * tile)
        summed = total[i] + got[0, i].astype(jnp.float32) + got[1, i].astype(jnp.float32)
        out_ref[:, cols] = (x_ref[:, cols].astype(jnp.float32) + summed).astype(out_ref.dtype)


def mix(query, keys, values, weight, x, tiles=4):
    toks, width = x.shape
    tile = width // tiles
    in_vmem = pl.BlockSpec(memory_space=pltpu.VMEM)
    return pl.pallas_call(
        mix_kernel,
        out_shape=jax.ShapeDtypeStruct(x.shape, jnp.bfloat16),
        in_specs=[in_vmem] * 5,
        out_specs=in_vmem,
        scratch_shapes=[
            pltpu.VMEM((toks, query.shape[1]), jnp.bfloat16),
            pltpu.VMEM((tiles, toks, tile), jnp.float32),
            pltpu.VMEM((3, tiles, toks, tile), jnp.bfloat16),
            pltpu.VMEM((3, tiles, toks, tile), jnp.bfloat16),
            pltpu.SemaphoreType.DMA((3, tiles)),
            pltpu.SemaphoreType.DMA((3, tiles)),
        ],
        compiler_params=pltpu.CompilerParams(
            collective_id=2, has_side_effects=True, vmem_limit_bytes=40 * MIB
        ),
        name="mix",
    )(query, keys, values, weight, x)


def attend(query, keys, values, rows=256):
    tokens, width = query.shape
    all_tokens = keys.shape[0]
    return pl.pallas_call(
        attend_kernel,
        out_shape=jax.ShapeDtypeStruct(query.shape, jnp.bfloat16),
        grid=(width // HD, tokens // rows),
        in_specs=[
            pl.BlockSpec((rows, HD), lambda h, i: (i, h)),
            pl.BlockSpec((all_tokens, HD), lambda h, i: (0, h)),
            pl.BlockSpec((all_tokens, HD), lambda h, i: (0, h)),
        ],
        out_specs=pl.BlockSpec((rows, HD), lambda h, i: (i, h)),
        compiler_params=pltpu.CompilerParams(vmem_limit_bytes=48 * MIB),
        name="attend",
    )(query, keys, values)


def general_embed(arrived, intersection_tiles, intersection, emb_weight, n_tensor):
    targets, depth, tile_rows, pix_block = intersection_tiles.shape
    _, channels, cell_rows = arrived.shape
    picked = jnp.take(arrived, intersection.reshape(-1), axis=0)
    tok_local = targets // 2
    half_tensor = n_tensor // 2
    sub_pix = pix_block // half_tensor
    picked = picked.reshape(tok_local, 2, depth, channels, cell_rows)
    tile_view = intersection_tiles.reshape(tok_local, 2, depth, tile_rows, half_tensor, sub_pix)
    numer = jnp.einsum("thkcr,thkrap->hactp", picked, tile_view, preferred_element_type=jnp.float32)
    area = jnp.sum(tile_view, axis=(2, 3), dtype=jnp.float32)
    area = jnp.transpose(area, (1, 2, 0, 3))[:, :, None]
    regridded = (numer / area).astype(jnp.bfloat16).reshape(n_tensor, channels, tok_local * sub_pix)
    moved = lax.all_to_all(regridded, "tensor", split_axis=0, concat_axis=2, tiled=True)
    pixels = moved.reshape(channels, n_tensor * tok_local, sub_pix)
    return jnp.einsum(
        "ctq,cqd->td", pixels, emb_weight, preferred_element_type=jnp.float32
    ).astype(jnp.bfloat16)


def general_project(own_rows, norm_gain, attention_in):
    values_f = own_rows.astype(jnp.float32)
    factor = lax.rsqrt(jnp.mean(values_f * values_f, axis=-1, keepdims=True) + EPS)
    normed = (values_f * factor * norm_gain).astype(jnp.bfloat16)
    normed = lax.all_gather(normed, "tensor", axis=0, tiled=True)

    def project(part):
        return jnp.dot(normed, attention_in[:, part], preferred_element_type=jnp.float32)

    keys = lax.all_gather(project(1).astype(jnp.bfloat16), "patch", axis=0, tiled=True)
    values = lax.all_gather(project(2).astype(jnp.bfloat16), "patch", axis=0, tiled=True)
    return (project(0) * HD ** (-0.5)).astype(jnp.bfloat16), keys, values


def on_device(
    source,
    intersection_tiles,
    send_index,
    intersection,
    emb_weight,
    norm_gain,
    attention_in,
    attention_out,
):
    n_tensor = lax.axis_size("tensor")
    blocks_here, channels, cell_rows = source.shape
    peers = send_index.shape[1]
    slots = send_index.shape[2]
    payload = jnp.take(source, send_index.reshape(-1), axis=0, mode="clip").reshape(
        peers, slots, channels, cell_rows
    )
    arrived = lax.all_to_all(payload, ("patch", "tensor"), split_axis=0, concat_axis=0, tiled=True)
    arrived = arrived.reshape(peers * slots, channels, cell_rows)
    if (
        2 * emb_weight.shape[1] == LANES
        and n_tensor == 4
        and lax.axis_size("patch") == 4
        and intersection_tiles.shape[0] % 32 == 0
    ):
        pixels = regrid(arrived, intersection_tiles, intersection.reshape(-1))
        own_rows = embed(pixels, emb_weight)
        query, keys, values = project_all(
            own_rows, norm_gain[None, :], jnp.transpose(attention_in, (1, 0, 2))
        )
        return mix(query, keys, values, attention_out, own_rows)
    partial = general_embed(arrived, intersection_tiles, intersection, emb_weight, n_tensor)
    own_rows = lax.psum_scatter(partial, "tensor", scatter_dimension=0, tiled=True)
    query, keys, values = general_project(own_rows, norm_gain, attention_in)
    heads_out = attend(query, keys, values)
    mixing = lax.psum_scatter(
        jnp.dot(heads_out, attention_out, preferred_element_type=jnp.float32).astype(jnp.bfloat16),
        "tensor",
        scatter_dimension=0,
        tiled=True,
    ).astype(jnp.float32)
    return (own_rows.astype(jnp.float32) + mixing).astype(jnp.bfloat16)


def solution(mesh):
    placed = (
        P(("groups", "patch", "tensor"), None, None),
        P(("patch", "tensor"), None, None, None),
        P(("patch", "tensor"), None, None),
        P(("patch", "tensor"), None),
        P(None, "tensor", None),
        P(),
        P(None, None, "tensor"),
        P("tensor", None),
    )
    return jax.shard_map(
        on_device,
        mesh=mesh,
        in_specs=placed,
        out_specs=P(("groups", "patch", "tensor"), None),
        check_vma=False,
    )
```

```python
import functools

import jax
import jax.numpy as jnp
from jax import lax
from jax.experimental import pallas as pl
from jax.experimental.pallas import tpu as pltpu
from jax.sharding import PartitionSpec as P

HD = 128
EPS = 1e-05
LANES = 128
MIB = 1 << 20


def round_up(value, unit):
    return -(-value // unit) * unit


def order_channels(arrived_ref, ordered):
    channels = arrived_ref.shape[1]
    pairs = (channels + 1) // 2
    half = ordered.shape[1] // 2
    row = lax.broadcasted_iota(jnp.int32, (2 * half, channels), 0)
    col = lax.broadcasted_iota(jnp.int32, (2 * half, channels), 1)
    wanted = jnp.where(row < half, 2 * row, 2 * (row - half) + 1)
    order = jnp.where(wanted == col, 1.0, 0.0).astype(jnp.bfloat16)
    place = lax.broadcasted_iota(jnp.int32, (2 * half, LANES), 0)
    valid = (place < pairs) | ((place >= half) & (place < half + channels // 2))

    @pl.loop(0, arrived_ref.shape[0])
    def _(slot):
        moved = jnp.dot(order, arrived_ref[slot], preferred_element_type=jnp.float32)
        moved = jnp.where(valid, moved, jnp.where(place == pairs, 1.0, 0.0))
        ordered[slot] = moved.astype(jnp.bfloat16)


def regrid(step, slot_ref, ordered, tiles, stage):
    half = ordered.shape[1] // 2
    toks = tiles.shape[0] // 2
    pairs = stage.shape[0] // (4 * toks)
    low = lax.broadcasted_iota(jnp.int32, (half, LANES), 1) < LANES // 2
    for tok in range(toks):
        for side in range(2):
            block = tok * 2 + side
            base = (step * toks * 2 + block) * 2
            lhs = jnp.concatenate([ordered[slot_ref[base]], ordered[slot_ref[base + 1]]], axis=1)
            rhs = tiles[block].reshape(2 * tiles.shape[2], LANES)
            numer = jnp.dot(lhs, rhs, preferred_element_type=jnp.float32)
            value = numer * (1.0 / numer[pairs : pairs + 1])
            even, odd = value[:half], value[half:]
            first = jnp.where(low, even, pltpu.roll(odd, LANES // 2, 1))
            second = jnp.where(low, pltpu.roll(even, LANES // 2, 1), odd)
            start = 2 * side * pairs * toks + tok
            stage[pl.ds(start, pairs, stride=toks), :] = first[:pairs]
            stage[pl.ds(start + pairs * toks, pairs, stride=toks), :] = second[:pairs]
    return stage[...].reshape(4, pairs, toks, LANES).astype(jnp.bfloat16)


def peer_of(axis, far):
    me = lax.axis_index(axis)
    if far == 1:
        return me + 1 - 2 * lax.rem(me, 2)
    if far == 2:
        return lax.rem(me + 2, 4)
    return 3 - me


def greet(pairs_of):
    barrier = pltpu.get_barrier_semaphore()
    for axis, far in pairs_of:
        pl.semaphore_signal(
            barrier,
            inc=1,
            device_id={axis: peer_of(axis, far)},
            device_id_type=pl.DeviceIdType.MESH,
        )
    pl.semaphore_wait(barrier, len(pairs_of))


def push(src, dst, send, recv, axis, far):
    return pltpu.make_async_remote_copy(
        src_ref=src,
        dst_ref=dst,
        send_sem=send,
        recv_sem=recv,
        device_id={axis: peer_of(axis, far)},
        device_id_type=pl.DeviceIdType.MESH,
    )


def embed_kernel(
    channels,
    slot_ref,
    arrived_ref,
    tiles_ref,
    w_ref,
    out_ref,
    ordered,
    tile_buf,
    stage,
    px,
    recv,
    w,
    lhs,
    part,
    got,
    total,
    local_sem,
    tile_sem,
    send_sem,
    recv_sem,
    part_send,
    part_recv,
):
    _, pairs, toks, _ = px.shape
    tiles, _, tile = total.shape
    chunk_blocks = tile_buf.shape[1]
    chunk = chunk_blocks // 2
    steps = toks // chunk
    me = lax.axis_index("tensor")

    def fetch(step):
        blocks = pl.ds(step * chunk_blocks, chunk_blocks)
        slot = lax.rem(step, 2)
        return pltpu.make_async_copy(tiles_ref.at[blocks], tile_buf.at[slot], tile_sem.at[slot])

    def move(far, step):
        rows = pl.ds(pl.multiple_of(step * chunk, chunk), chunk)
        return push(
            px.at[peer_of("tensor", far), :, rows],
            recv.at[far - 1, :, rows],
            send_sem.at[far - 1, step],
            recv_sem.at[far - 1, step],
            "tensor",
            far,
        )

    fetch(jnp.int32(0)).start()
    if channels < 2 * pairs:
        w[channels:] = jnp.zeros((2 * pairs - channels,) + w.shape[1:], w.dtype)
    order_channels(arrived_ref, ordered)
    greet([("tensor", far) for far in (1, 2, 3)])

    @pl.loop(0, steps)
    def _(step):
        @pl.when(step + 1 < steps)
        def _():
            fetch(step + 1).start()

        fetch(step).wait()
        rows = pl.ds(pl.multiple_of(step * chunk, chunk), chunk)
        px[:, :, rows] = regrid(step, slot_ref, ordered, tile_buf.at[lax.rem(step, 2)], stage)
        move(3, step).start()
        move(1, step).start()

    load = pltpu.make_async_copy(w_ref, w.at[pl.ds(0, channels)], local_sem)
    load.start()

    def back(far, i):
        return push(
            part.at[far - 1, i],
            got.at[far - 1, i],
            part_send.at[far - 1, i],
            part_recv.at[far - 1, i],
            "tensor",
            2 if far == 2 else 1,
        )

    def multiply(far):
        @pl.loop(0, pairs)
        def _(j):
            block = px[me, j] if far == 0 else recv[far - 1, j]
            lhs[:, pl.ds(pl.multiple_of(j * LANES, LANES), LANES)] = block

        @pl.loop(0, tiles)
        def _(i):
            cols = pl.ds(pl.multiple_of(i * tile, tile), tile)
            rhs = w[:, :, cols].reshape(pairs * LANES, tile)
            summed = jnp.dot(lhs[...], rhs, preferred_element_type=jnp.float32)
            if far == 0:
                total[i] = summed
            else:
                if far == 2:
                    back(3, i).wait_recv()
                    summed += got[2, i].astype(jnp.float32)
                part[far - 1, i] = summed.astype(part.dtype)
                back(far, i).start()

    load.wait()
    multiply(0)

    @pl.loop(0, steps)
    def _(step):
        move(3, step).wait_send()
        move(2, step).start()

    for far in (3, 1, 2):

        @pl.loop(0, steps)
        def _(step):
            move(far, step).wait_recv()

        multiply(far)

    @pl.loop(0, steps)
    def _(step):
        move(1, step).wait_send()
        move(2, step).wait_send()

    @pl.loop(0, tiles)
    def _(i):
        back(3, i).wait_send()
        summed = total[i]
        for far in (1, 2):
            back(far, i).wait()
            summed += got[far - 1, i].astype(jnp.float32)
        cols = pl.ds(pl.multiple_of(i * tile, tile), tile)
        out_ref[:, cols] = summed.astype(out_ref.dtype)


def embed(slots, arrived, intersection_tiles, weight, chunk=16, tile=512):
    channels, sub_pix, width = weight.shape
    n_slots, _, cells = arrived.shape
    toks = intersection_tiles.shape[0] // 2
    pairs = (channels + 1) // 2
    half = round_up(pairs + 1, 8)
    tiles = width // tile
    steps = toks // chunk
    return pl.pallas_call(
        functools.partial(embed_kernel, channels),
        out_shape=jax.ShapeDtypeStruct((toks, width), jnp.bfloat16),
        in_specs=[
            pl.BlockSpec(memory_space=pltpu.SMEM),
            pl.BlockSpec(memory_space=pltpu.VMEM),
            pl.BlockSpec(memory_space=pl.ANY),
            pl.BlockSpec(memory_space=pl.ANY),
        ],
        out_specs=pl.BlockSpec(memory_space=pltpu.VMEM),
        scratch_shapes=[
            pltpu.VMEM((n_slots, 2 * half, cells), jnp.bfloat16),
            pltpu.VMEM((2, 2 * chunk) + intersection_tiles.shape[1:], jnp.bfloat16),
            pltpu.VMEM((4 * pairs * chunk, LANES), jnp.float32),
            pltpu.VMEM((4, pairs, toks, LANES), jnp.bfloat16),
            pltpu.VMEM((3, pairs, toks, LANES), jnp.bfloat16),
            pltpu.VMEM((2 * pairs, sub_pix, width), jnp.bfloat16),
            pltpu.VMEM((toks, pairs * LANES), jnp.bfloat16),
            pltpu.VMEM((3, tiles, toks, tile), jnp.bfloat16),
            pltpu.VMEM((3, tiles, toks, tile), jnp.bfloat16),
            pltpu.VMEM((tiles, toks, tile), jnp.float32),
            pltpu.SemaphoreType.DMA,
            pltpu.SemaphoreType.DMA((2,)),
            pltpu.SemaphoreType.DMA((3, steps)),
            pltpu.SemaphoreType.DMA((3, steps)),
            pltpu.SemaphoreType.DMA((3, tiles)),
            pltpu.SemaphoreType.DMA((3, tiles)),
        ],
        compiler_params=pltpu.CompilerParams(
            collective_id=0, has_side_effects=True, vmem_limit_bytes=54 * MIB
        ),
        name="embed",
    )(slots, arrived, intersection_tiles, weight)


def project_kernel(
    x_ref,
    gain_ref,
    w_ref,
    q_ref,
    k_ref,
    v_ref,
    rows,
    w,
    load_sem,
    row_send,
    row_recv,
    key_send,
    key_recv,
    value_send,
    value_recv,
):
    load = pltpu.make_async_copy(w_ref, w, load_sem)
    load.start()
    values = x_ref[...].astype(jnp.float32)
    factor = lax.rsqrt(jnp.mean(values * values, axis=-1, keepdims=True) + EPS)
    rows[0] = (values * factor * gain_ref[...]).astype(jnp.bfloat16)
    toks = rows.shape[1]
    greet([("tensor", 1), ("tensor", 2), ("patch", 1), ("patch", 2)])

    def row_move(src, dst, far):
        return push(rows.at[src], rows.at[dst], row_send.at[dst], row_recv.at[dst], "tensor", far)

    across = row_move(0, 2, 2)
    beside = row_move(0, 1, 1)
    relay = row_move(2, 3, 1)
    across.start()
    beside.start()
    load.wait()

    def cross(block, src, dst, far):
        return [
            push(
                ref.at[src, block],
                ref.at[dst, block],
                sent.at[dst, block],
                came.at[dst, block],
                "patch",
                far,
            )
            for ref, sent, came in (
                (k_ref, key_send, key_recv),
                (v_ref, value_send, value_recv),
            )
        ]

    def project(block):
        x = rows[block]
        k_ref[0, block] = jnp.dot(x, w[1], preferred_element_type=jnp.float32).astype(jnp.bfloat16)
        v_ref[0, block] = jnp.dot(x, w[2], preferred_element_type=jnp.float32).astype(jnp.bfloat16)
        for copy in cross(block, 0, 2, 2) + cross(block, 0, 1, 1):
            copy.start()
        query = jnp.dot(x, w[0], preferred_element_type=jnp.float32) * HD ** (-0.5)
        place = lax.axis_index("tensor") if block == 0 else peer_of("tensor", block)
        q_ref[pl.ds(pl.multiple_of(place * toks, toks), toks), :] = query.astype(jnp.bfloat16)

    project(0)
    across.wait_recv()
    relay.start()
    project(2)
    beside.wait_recv()
    project(1)
    for block in (0, 2):
        for copy in cross(block, 0, 2, 2):
            copy.wait_recv()
        for copy in cross(block, 2, 3, 1):
            copy.start()
    relay.wait_recv()
    project(3)
    for block in (1, 3):
        for copy in cross(block, 0, 2, 2):
            copy.wait_recv()
        for copy in cross(block, 2, 3, 1):
            copy.start()
    for block in range(4):
        for copy in cross(block, 0, 1, 1) + cross(block, 2, 3, 1):
            copy.wait()
        for copy in cross(block, 0, 2, 2):
            copy.wait_send()
    for copy in (across, beside, relay):
        copy.wait_send()


def project_all(x, gain, weight):
    toks, width = x.shape
    heads_width = weight.shape[2]
    kept = jax.ShapeDtypeStruct((4, 4, toks, heads_width), jnp.bfloat16)
    in_vmem = pl.BlockSpec(memory_space=pltpu.VMEM)
    query, keys, values = pl.pallas_call(
        project_kernel,
        out_shape=(jax.ShapeDtypeStruct((4 * toks, heads_width), jnp.bfloat16), kept, kept),
        in_specs=[in_vmem, in_vmem, pl.BlockSpec(memory_space=pl.ANY)],
        out_specs=(in_vmem, in_vmem, in_vmem),
        scratch_shapes=[
            pltpu.VMEM((4, toks, width), jnp.bfloat16),
            pltpu.VMEM(weight.shape, jnp.bfloat16),
            pltpu.SemaphoreType.DMA,
            pltpu.SemaphoreType.DMA((4,)),
            pltpu.SemaphoreType.DMA((4,)),
        ]
        + [pltpu.SemaphoreType.DMA((4, 4))] * 4,
        compiler_params=pltpu.CompilerParams(
            collective_id=1, has_side_effects=True, vmem_limit_bytes=40 * MIB
        ),
        name="project_all",
    )(x, gain, weight)
    return query, keys.reshape(-1, heads_width), values.reshape(-1, heads_width)


def attend_rows(query, keys, values):
    scores = lax.dot_general(
        query, keys, (((1,), (1,)), ((), ())), preferred_element_type=jnp.float32
    )
    highest = jnp.max(scores, axis=-1, keepdims=True)
    expo = jnp.exp(scores - highest)
    denom = jnp.sum(expo, axis=-1, keepdims=True)
    summed = jnp.dot(expo.astype(jnp.bfloat16), values, preferred_element_type=jnp.float32)
    return (summed / denom).astype(jnp.bfloat16)


def attend_kernel(q_ref, k_ref, v_ref, out_ref):
    out_ref[...] = attend_rows(q_ref[...], k_ref[...], v_ref[...])


def mix_kernel(
    q_ref, k_ref, v_ref, w_ref, x_ref, out_ref, heads, total, part, got, send_sem, recv_sem
):
    _, tiles, toks, tile = part.shape

    def back(far, i):
        return push(
            part.at[far - 1, i],
            got.at[far - 1, i],
            send_sem.at[far - 1, i],
            recv_sem.at[far - 1, i],
            "tensor",
            2 if far == 2 else 1,
        )

    def attended(far):
        place = lax.axis_index("tensor") if far == 0 else peer_of("tensor", far)
        rows = pl.ds(pl.multiple_of(place * toks, toks), toks)
        for head in range(heads.shape[1] // HD):
            lanes = slice(head * HD, (head + 1) * HD)
            heads[:, lanes] = attend_rows(q_ref[rows, lanes], k_ref[:, lanes], v_ref[:, lanes])

    def mixed(i):
        cols = slice(i * tile, (i + 1) * tile)
        return jnp.dot(heads[...], w_ref[:, cols], preferred_element_type=jnp.float32)

    greet([("tensor", 1), ("tensor", 2)])
    attended(3)
    for i in range(tiles):
        part[2, i] = mixed(i).astype(part.dtype)
        back(3, i).start()
    attended(2)
    for i in range(tiles):
        total[i] = mixed(i)
    attended(1)
    for i in range(tiles):
        part[0, i] = mixed(i).astype(part.dtype)
    for i in range(tiles):
        back(3, i).wait_recv()
        part[1, i] = (total[i] + got[2, i].astype(jnp.float32)).astype(part.dtype)
        back(2, i).start()
        back(1, i).start()
    attended(0)
    for i in range(tiles):
        total[i] = mixed(i)
    for i in range(tiles):
        back(3, i).wait_send()
        back(1, i).wait()
        back(2, i).wait()
        cols = slice(i * tile, (i + 1) * tile)
        summed = total[i] + got[0, i].astype(jnp.float32) + got[1, i].astype(jnp.float32)
        out_ref[:, cols] = (x_ref[:, cols].astype(jnp.float32) + summed).astype(out_ref.dtype)


def mix(query, keys, values, weight, x, tiles=4):
    toks, width = x.shape
    tile = width // tiles
    in_vmem = pl.BlockSpec(memory_space=pltpu.VMEM)
    return pl.pallas_call(
        mix_kernel,
        out_shape=jax.ShapeDtypeStruct(x.shape, jnp.bfloat16),
        in_specs=[in_vmem] * 5,
        out_specs=in_vmem,
        scratch_shapes=[
            pltpu.VMEM((toks, query.shape[1]), jnp.bfloat16),
            pltpu.VMEM((tiles, toks, tile), jnp.float32),
            pltpu.VMEM((3, tiles, toks, tile), jnp.bfloat16),
            pltpu.VMEM((3, tiles, toks, tile), jnp.bfloat16),
            pltpu.SemaphoreType.DMA((3, tiles)),
            pltpu.SemaphoreType.DMA((3, tiles)),
        ],
        compiler_params=pltpu.CompilerParams(
            collective_id=2, has_side_effects=True, vmem_limit_bytes=40 * MIB
        ),
        name="mix",
    )(query, keys, values, weight, x)


def attend(query, keys, values, rows=256):
    tokens, width = query.shape
    all_tokens = keys.shape[0]
    return pl.pallas_call(
        attend_kernel,
        out_shape=jax.ShapeDtypeStruct(query.shape, jnp.bfloat16),
        grid=(width // HD, tokens // rows),
        in_specs=[
            pl.BlockSpec((rows, HD), lambda h, i: (i, h)),
            pl.BlockSpec((all_tokens, HD), lambda h, i: (0, h)),
            pl.BlockSpec((all_tokens, HD), lambda h, i: (0, h)),
        ],
        out_specs=pl.BlockSpec((rows, HD), lambda h, i: (i, h)),
        compiler_params=pltpu.CompilerParams(vmem_limit_bytes=48 * MIB),
        name="attend",
    )(query, keys, values)


def general_embed(arrived, intersection_tiles, intersection, emb_weight, n_tensor):
    targets, depth, tile_rows, pix_block = intersection_tiles.shape
    _, channels, cell_rows = arrived.shape
    picked = jnp.take(arrived, intersection.reshape(-1), axis=0)
    tok_local = targets // 2
    half_tensor = n_tensor // 2
    sub_pix = pix_block // half_tensor
    picked = picked.reshape(tok_local, 2, depth, channels, cell_rows)
    tile_view = intersection_tiles.reshape(tok_local, 2, depth, tile_rows, half_tensor, sub_pix)
    numer = jnp.einsum("thkcr,thkrap->hactp", picked, tile_view, preferred_element_type=jnp.float32)
    area = jnp.sum(tile_view, axis=(2, 3), dtype=jnp.float32)
    area = jnp.transpose(area, (1, 2, 0, 3))[:, :, None]
    regridded = (numer / area).astype(jnp.bfloat16).reshape(n_tensor, channels, tok_local * sub_pix)
    moved = lax.all_to_all(regridded, "tensor", split_axis=0, concat_axis=2, tiled=True)
    pixels = moved.reshape(channels, n_tensor * tok_local, sub_pix)
    return jnp.einsum(
        "ctq,cqd->td", pixels, emb_weight, preferred_element_type=jnp.float32
    ).astype(jnp.bfloat16)


def general_project(own_rows, norm_gain, attention_in):
    values_f = own_rows.astype(jnp.float32)
    factor = lax.rsqrt(jnp.mean(values_f * values_f, axis=-1, keepdims=True) + EPS)
    normed = (values_f * factor * norm_gain).astype(jnp.bfloat16)
    normed = lax.all_gather(normed, "tensor", axis=0, tiled=True)

    def project(part):
        return jnp.dot(normed, attention_in[:, part], preferred_element_type=jnp.float32)

    keys = lax.all_gather(project(1).astype(jnp.bfloat16), "patch", axis=0, tiled=True)
    values = lax.all_gather(project(2).astype(jnp.bfloat16), "patch", axis=0, tiled=True)
    return (project(0) * HD ** (-0.5)).astype(jnp.bfloat16), keys, values


def on_device(
    source,
    intersection_tiles,
    send_index,
    intersection,
    emb_weight,
    norm_gain,
    attention_in,
    attention_out,
):
    n_tensor = lax.axis_size("tensor")
    blocks_here, channels, cell_rows = source.shape
    peers = send_index.shape[1]
    slots = send_index.shape[2]
    payload = jnp.take(source, send_index.reshape(-1), axis=0, mode="clip").reshape(
        peers, slots, channels, cell_rows
    )
    arrived = lax.all_to_all(payload, ("patch", "tensor"), split_axis=0, concat_axis=0, tiled=True)
    arrived = arrived.reshape(peers * slots, channels, cell_rows)
    if (
        2 * emb_weight.shape[1] == LANES
        and n_tensor == 4
        and lax.axis_size("patch") == 4
        and intersection_tiles.shape[0] % 32 == 0
    ):
        own_rows = embed(intersection.reshape(-1), arrived, intersection_tiles, emb_weight)
        query, keys, values = project_all(
            own_rows, norm_gain[None, :], jnp.transpose(attention_in, (1, 0, 2))
        )
        return mix(query, keys, values, attention_out, own_rows)
    partial = general_embed(arrived, intersection_tiles, intersection, emb_weight, n_tensor)
    own_rows = lax.psum_scatter(partial, "tensor", scatter_dimension=0, tiled=True)
    query, keys, values = general_project(own_rows, norm_gain, attention_in)
    heads_out = attend(query, keys, values)
    mixing = lax.psum_scatter(
        jnp.dot(heads_out, attention_out, preferred_element_type=jnp.float32).astype(jnp.bfloat16),
        "tensor",
        scatter_dimension=0,
        tiled=True,
    ).astype(jnp.float32)
    return (own_rows.astype(jnp.float32) + mixing).astype(jnp.bfloat16)


def solution(mesh):
    placed = (
        P(("groups", "patch", "tensor"), None, None),
        P(("patch", "tensor"), None, None, None),
        P(("patch", "tensor"), None, None),
        P(("patch", "tensor"), None),
        P(None, "tensor", None),
        P(),
        P(None, None, "tensor"),
        P("tensor", None),
    )
    return jax.shard_map(
        on_device,
        mesh=mesh,
        in_specs=placed,
        out_specs=P(("groups", "patch", "tensor"), None),
        check_vma=False,
    )
```
